128 devices in a mesh: dp: 8 (over z_hi, x), vocab: 16 (over y, z_lo, core).
Axes of the slice: x: 4, y: 4, z: 4 (z_hi: 2, z_lo: 2; z = z_hi * 2 + z_lo), core: 2. Of those that a mesh axis runs over, the one named last changes fastest.
Arguments:
- hidden: bfloat16 [1024, 3584], P('dp'), may hold values from -60 to 60
- head_weight: bfloat16 [3584, 131072], P(None, ('dp', 'vocab')), may hold values from -1 to 1
- teacher_logits: bfloat16 [1024, 131072], P('vocab', 'dp'), may hold values from -30 to 30
Outputs:
- grad_hidden: bfloat16 [1024, 3584], P(('dp', 'vocab'))
- grad_head: bfloat16 [3584, 131072], P(None, ('dp', 'vocab'))
The draws below stay inside these ranges and needn't reach their ends.
All inputs are finite; a program needn't handle non-finite values.
Results may differ from the reference program's by a relative error of at most 0.015.
Values may be sent and summed in bfloat16 or wider, within the bound.
No kernel may reach another device: no remote copies, remote signals or barrier semaphores. Data moves between devices by JAX's collectives and lax.ppermute only.
A program may use at most 128 MiB of HBM per device.

```python
import math
import jax
import jax.numpy as jnp
from jax import lax

D = 3584
V = 131072
ROWS = 1024


def draw_hidden(key, part):
    key = jax.random.fold_in(key, 11)
    first, second = jax.random.split(key)
    values = jnp.clip(jax.random.normal(first, (ROWS, D), jnp.float32), -6.0, 6.0)
    scales = jnp.exp(jax.random.uniform(second, (ROWS, 1), jnp.float32, 0.0, math.log(10.0)))
    return jnp.clip(values * scales, -60.0, 60.0).astype(jnp.bfloat16)


def draw_head_weight(key, part):
    key = jax.random.fold_in(key, 12)
    first, second = jax.random.split(key)
    values = jnp.clip(jax.random.normal(first, (D, V), jnp.float32), -6.0, 6.0)
    column = jnp.exp(jax.random.uniform(second, (1, V), jnp.float32, 0.0, math.log(10.0))) / math.sqrt(10.0)
    return jnp.clip(values * column * D ** (-0.5), -1.0, 1.0).astype(jnp.bfloat16)


def draw_teacher_logits(key, part):
    key = jax.random.fold_in(key, 13)
    first, second, third = jax.random.split(key, 3)
    ramp = jnp.arange(V, dtype=jnp.float32) / V
    column = jnp.exp(jax.random.uniform(second, (1, V), jnp.float32, 0.0, math.log(10.0)))
    rows = jnp.exp(jax.random.uniform(third, (ROWS, 1), jnp.float32, 0.0, math.log(3.0)))
    values = jax.random.normal(first, (ROWS, V), jnp.float32)
    offset = 2.0 * math.log(3.0) * ramp
    return (30.0 * jnp.tanh((values * rows * column + offset[None, :]) / 30.0)).astype(jnp.bfloat16)


def setup_inputs(seed: int = 0) -> dict:
    key_of = jax.random.split(jax.random.key(seed), 4)
    return {
        "hidden": draw_hidden(jax.random.fold_in(key_of[3], 71), 0),
        "head_weight": draw_head_weight(jax.random.fold_in(key_of[3], 71), 0),
        "teacher_logits": draw_teacher_logits(jax.random.fold_in(key_of[3], 71), 0),
    }


def reference(hidden, head_weight, teacher_logits):
    raw = jnp.dot(hidden, head_weight, preferred_element_type=jnp.float32)
    capped = jnp.tanh(raw / 30.0)
    student = 30.0 * capped
    student_exp = jnp.exp(student / 2.0)
    teacher_exp = jnp.exp(teacher_logits.astype(jnp.float32) / 2.0)
    student_total = jnp.sum(student_exp, axis=1, keepdims=True)
    teacher_total = jnp.sum(teacher_exp, axis=1, keepdims=True)
    student_prob = student_exp / student_total
    teacher_prob = teacher_exp / teacher_total
    delta = (4096.0 * 2.0 * (student_prob - teacher_prob) * (1.0 - capped * capped)).astype(jnp.bfloat16)
    grad_hidden = lax.dot_general(delta, head_weight, (((1,), (1,)), ((), ())), preferred_element_type=jnp.float32)
    grad_head = lax.dot_general(hidden, delta, (((0,), (0,)), ((), ())), preferred_element_type=jnp.float32)
    return grad_hidden.astype(jnp.bfloat16), grad_head.astype(jnp.bfloat16)
```

```python
import jax
import jax.numpy as jnp
from jax import lax
from jax.sharding import Mesh, PartitionSpec as P

BF = jnp.bfloat16
F32 = jnp.float32
CHIPS = ("zh", "x", "y", "zl")
Z = ("zh", "zl")


def shift(v, axis, size, step):
    return lax.ppermute(v, axis, [(i, (i + step) % size) for i in range(size)])


def swap(v):
    return shift(v, "core", 2, 1)


def total(v):
    v = v + swap(v)
    for axis in ("x", "y", Z):
        v = v + shift(v, axis, 4, 1) + shift(v, axis, 4, 3) + shift(v, axis, 4, 2)
    return v


def gather_rows(own):
    far = shift(own, "zh", 2, 1)
    zh, x = lax.axis_index("zh"), lax.axis_index("x")
    rows, cols = own.shape
    out = jnp.zeros((8, rows, cols), own.dtype)
    for block, hi in ((own, zh), (far, 1 - zh)):
        for step in (0, 1, 3, 2):
            moved = block if step == 0 else shift(block, "x", 4, step)
            out = lax.dynamic_update_index_in_dim(out, moved, hi * 4 + (x - step) % 4, 0)
    return out.reshape(8 * rows, cols)


def per_device(hidden, head_weight, teacher_logits):
    core = lax.axis_index("core")
    half = hidden.shape[1] // 2
    own = gather_rows(lax.dynamic_slice_in_dim(hidden, core * half, half, 1))
    teacher = lax.all_to_all(
        teacher_logits, ("y", "zl", "core"), split_axis=1, concat_axis=0, tiled=True
    )
    other = swap(own)
    gathered = jnp.where(
        core == 0, jnp.concatenate([own, other], 1), jnp.concatenate([other, own], 1)
    )
    raw = jnp.dot(gathered, head_weight, preferred_element_type=F32)
    capped = jnp.tanh(raw / 30.0)
    student_exp = jnp.exp(15.0 * capped)
    teacher_exp = jnp.exp(teacher.astype(F32) / 2.0)
    totals = total(jnp.stack([jnp.sum(student_exp, axis=1), jnp.sum(teacher_exp, axis=1)]))
    student_prob = student_exp / totals[0][:, None]
    teacher_prob = teacher_exp / totals[1][:, None]
    delta = (4096.0 * 2.0 * (student_prob - teacher_prob) * (1.0 - capped * capped)).astype(BF)
    share = lax.dot_general(
        delta, head_weight, (((1,), (1,)), ((), ())), preferred_element_type=F32
    ).astype(BF)
    keep = lax.dynamic_slice_in_dim(share, core * half, half, 1)
    give = lax.dynamic_slice_in_dim(share, (1 - core) * half, half, 1)
    chip = (keep.astype(F32) + swap(give).astype(F32)).astype(BF)
    chip = lax.all_to_all(chip, CHIPS, split_axis=0, concat_axis=0, tiled=True)
    chip = jnp.sum(chip.reshape(64, 16, half).astype(F32), axis=0).astype(BF)
    mine = lax.dynamic_slice_in_dim(chip, core * 8, 8, 0)
    rest = swap(lax.dynamic_slice_in_dim(chip, (1 - core) * 8, 8, 0))
    grad_hidden = jnp.where(
        core == 0, jnp.concatenate([mine, rest], 1), jnp.concatenate([rest, mine], 1)
    )
    grad_head = lax.dot_general(
        gathered, delta, (((0,), (0,)), ((), ())), preferred_element_type=F32
    )
    return grad_hidden, grad_head.astype(BF)


def solution(mesh):
    fine = Mesh(mesh.devices.reshape(2, 4, 4, 2, 2), ("zh", "x", "y", "zl", "core"))
    dp, vocab = ("zh", "x"), ("y", "zl", "core")
    return jax.shard_map(
        per_device,
        mesh=fine,
        in_specs=(P(dp, None), P(None, dp + vocab), P(vocab, dp)),
        out_specs=(P(dp + vocab, None), P(None, dp + vocab)),
        check_vma=False,
    )
```

```python
import functools

import jax
import jax.numpy as jnp
from jax import lax
from jax.experimental import pallas as pl
from jax.experimental.pallas import tpu as pltpu
from jax.sharding import Mesh, PartitionSpec as P

BF = jnp.bfloat16
F32 = jnp.float32
CHIPS = ("zh", "x", "y", "zl")
Z = ("zh", "zl")
SMEM = pl.BlockSpec(memory_space=pltpu.SMEM)
VMEM = pl.BlockSpec(memory_space=pltpu.VMEM)
ANY = pl.BlockSpec(memory_space=pl.ANY)


def shift(v, axis, size, step):
    return lax.ppermute(v, axis, [(i, (i + step) % size) for i in range(size)])


def swap(v):
    return shift(v, "core", 2, 1)


def total(v):
    v = v + swap(v)
    for axis in ("x", "y", Z):
        v = v + shift(v, axis, 4, 1) + shift(v, axis, 4, 3) + shift(v, axis, 4, 2)
    return v


def scores_kernel(tile, place, hidden, *refs):
    blocks, (weight, teacher_sum, gathered, capped, sums) = refs[:14], refs[14:19]
    rows_v, weight_v, capped_v, part, row_sem, weight_sem, out_sem, capped_sem = refs[19:]
    rows, half = blocks[0].shape
    own = pl.multiple_of(place[8] * half, half)
    other = pl.multiple_of((1 - place[8]) * half, half)
    loads = []
    for i in range(8):
        at = pl.ds(pl.multiple_of(place[i] * rows, rows), rows)
        if i == 0:
            loads.append((hidden, rows_v.at[at, :]))
        else:
            loads.append((blocks[i - 1], rows_v.at[at, pl.ds(own, half)]))
            loads.append((blocks[i + 6], rows_v.at[at, pl.ds(other, half)]))
    loads = [pltpu.make_async_copy(a, b, row_sem.at[i]) for i, (a, b) in enumerate(loads)]
    count = weight.shape[1] // tile
    cols = [slice(n * tile, (n + 1) * tile) for n in range(count)]
    weights = [
        pltpu.make_async_copy(weight.at[:, c], weight_v.at[:, c], weight_sem.at[n])
        for n, c in enumerate(cols)
    ]
    weights[0].start()
    for c in loads:
        c.start()
    for c in weights[1:]:
        c.start()
    for c in loads:
        c.wait()
    keep = pltpu.make_async_copy(rows_v, gathered, out_sem)
    keep.start()
    part[...] = jnp.zeros_like(part)
    stores = []
    for n, c in enumerate(cols):
        weights[n].wait()

        @pl.loop(0, rows_v.shape[0] // 512)
        def _(m):
            at = pl.ds(pl.multiple_of(m * 512, 512), 512)
            raw = jnp.dot(rows_v[at, :], weight_v[:, c], preferred_element_type=F32)
            cap = jnp.tanh(raw / 30.0)
            capped_v[at, c] = cap
            e = jnp.exp(15.0 * cap)
            s = part[at, :]
            for k in range(tile // 128):
                s = s + e[:, k * 128 : (k + 1) * 128]
            part[at, :] = s

        stores.append(
            pltpu.make_async_copy(capped_v.at[:, c], capped.at[:, c], capped_sem.at[n])
        )
        stores[-1].start()
    sums[0:1, :] = jnp.sum(part[...].T, axis=0, keepdims=True)
    sums[1:2, :] = teacher_sum[...]
    for c in stores + [keep]:
        c.wait()


def scores(place, hidden, own, other, weight, teacher_sum):
    rows, depth, cols, tile = 8 * hidden.shape[0], *weight.shape, 256
    return pl.pallas_call(
        functools.partial(scores_kernel, tile),
        name="scores",
        out_shape=(
            jax.ShapeDtypeStruct((rows, depth), BF),
            jax.ShapeDtypeStruct((rows, cols), F32),
            jax.ShapeDtypeStruct((2, rows), F32),
        ),
        in_specs=[SMEM, ANY] + [ANY] * 14 + [ANY, VMEM],
        out_specs=(ANY, ANY, VMEM),
        scratch_shapes=[
            pltpu.VMEM((rows, depth), BF),
            pltpu.VMEM((depth, cols), BF),
            pltpu.VMEM((rows, cols), F32),
            pltpu.VMEM((rows, 128), F32),
            pltpu.SemaphoreType.DMA((15,)),
            pltpu.SemaphoreType.DMA((cols // tile,)),
            pltpu.SemaphoreType.DMA,
            pltpu.SemaphoreType.DMA((cols // tile,)),
        ],
        compiler_params=pltpu.CompilerParams(vmem_limit_bytes=40 << 20),
        cost_estimate=pl.CostEstimate(
            flops=2 * rows * depth * cols, bytes_accessed=20 << 20, transcendentals=2 * rows * cols
        ),
    )(place, hidden, *own, *other, weight, teacher_sum)


def delta_kernel(core, capped, teacher, totals, weight, delta, share):
    scale = (8192.0 / totals[...]).T
    cap = capped[...]
    student = jnp.exp(15.0 * cap) * scale[:, 0:1]
    target = jnp.exp(teacher[...].astype(F32) * 0.5) * scale[:, 1:2]
    d = ((student - target) * (1.0 - cap * cap)).astype(BF)
    delta[...] = d
    share[...] = lax.dot_general(
        d, weight[...], (((1,), (1,)), ((), ())), preferred_element_type=F32
    ).astype(BF)


def delta_and_share(core, capped, teacher, totals, weight):
    (rows, cols), half, tile = capped.shape, weight.shape[0] // 2, 256
    block = lambda shape, f: pl.BlockSpec(shape, f)
    return pl.pallas_call(
        delta_kernel,
        name="delta_and_share",
        grid_spec=pltpu.PrefetchScalarGridSpec(
            num_scalar_prefetch=1,
            grid=(rows // tile,),
            in_specs=[
                block((tile, cols), lambda i, core: (i, 0)),
                block((tile, cols), lambda i, core: (i, 0)),
                block((8, tile), lambda i, core: (0, i)),
                block((half, cols), lambda i, core: (1 - core[0], 0)),
            ],
            out_specs=[
                block((tile, cols), lambda i, core: (i, 0)),
                block((tile, half), lambda i, core: (i, 0)),
            ],
        ),
        out_shape=(
            jax.ShapeDtypeStruct((rows, cols), BF),
            jax.ShapeDtypeStruct((rows, half), BF),
        ),
        compiler_params=pltpu.CompilerParams(vmem_limit_bytes=40 << 20),
        cost_estimate=pl.CostEstimate(
            flops=2 * rows * half * cols, bytes_accessed=16 << 20, transcendentals=2 * rows * cols
        ),
    )(core, capped, teacher, totals, weight)


def share_kernel(core, delta, weight, share):
    share[...] = lax.dot_general(
        delta[...], weight[...], (((1,), (1,)), ((), ())), preferred_element_type=F32
    ).astype(BF)


def own_share(core, delta, weight):
    (rows, cols), half, tile = delta.shape, weight.shape[0] // 2, 256
    return pl.pallas_call(
        share_kernel,
        name="own_share",
        grid_spec=pltpu.PrefetchScalarGridSpec(
            num_scalar_prefetch=1,
            grid=(rows // tile,),
            in_specs=[
                pl.BlockSpec((tile, cols), lambda i, core: (i, 0)),
                pl.BlockSpec((half, cols), lambda i, core: (core[0], 0)),
            ],
            out_specs=pl.BlockSpec((tile, half), lambda i, core: (i, 0)),
        ),
        out_shape=jax.ShapeDtypeStruct((rows, half), BF),
        compiler_params=pltpu.CompilerParams(vmem_limit_bytes=40 << 20),
        cost_estimate=pl.CostEstimate(
            flops=2 * rows * half * cols, bytes_accessed=10 << 20, transcendentals=0
        ),
    )(core, delta, weight)


def chip_sum_kernel(parts, after, out):
    out[...] = jnp.sum(parts[...].astype(F32), axis=0).astype(BF)


def chip_sum(parts, after):
    _, rows, cols = parts.shape
    tile = 256
    return pl.pallas_call(
        chip_sum_kernel,
        name="chip_sum",
        grid=(cols // tile,),
        in_specs=[pl.BlockSpec((parts.shape[0], rows, tile), lambda i: (0, 0, i)), ANY],
        out_specs=pl.BlockSpec((rows, tile), lambda i: (0, i)),
        out_shape=jax.ShapeDtypeStruct((rows, cols), BF),
        cost_estimate=pl.CostEstimate(flops=parts.size, bytes_accessed=4 << 20, transcendentals=0),
    )(parts, after)


def per_device(hidden, head_weight, teacher_logits):
    core = lax.axis_index("core")
    zh, x = lax.axis_index("zh"), lax.axis_index("x")
    vocab = lax.axis_index(("y", "zl", "core"))
    half = hidden.shape[1] // 2
    rows = 8 * hidden.shape[0]
    steps = (1, 3, 2)

    near = lax.dynamic_slice_in_dim(hidden, core * half, half, 1)
    far = shift(near, "zh", 2, 1)
    own = [shift(near, "x", 4, s) for s in steps]
    own += [far] + [shift(far, "x", 4, s) for s in steps]
    other = [swap(b) for b in own]
    place = [zh * 4 + (x - s) % 4 for s in (0,) + steps]
    place += [(1 - zh) * 4 + (x - s) % 4 for s in (0,) + steps]
    place = jnp.stack(place + [core]).astype(jnp.int32)

    teacher = lax.all_to_all(
        teacher_logits, ("y", "zl", "core"), split_axis=1, concat_axis=0, tiled=True
    )
    mine = jnp.sum(jnp.exp(teacher_logits.astype(F32) / 2.0), axis=1)
    teacher_sum = lax.dynamic_update_slice_in_dim(
        jnp.zeros((rows,), F32), mine, vocab * mine.shape[0], 0
    )
    gathered, capped, sums = scores(place, hidden, own, other, head_weight, teacher_sum[None])
    totals = jnp.concatenate([total(sums), jnp.ones((6, rows), F32)])

    which = core[None].astype(jnp.int32)
    delta, give = delta_and_share(which, capped, teacher, totals, head_weight)
    keep = own_share(which, delta, head_weight)
    chip = (keep.astype(F32) + swap(give).astype(F32)).astype(BF)
    parts = lax.all_to_all(chip, CHIPS, split_axis=0, concat_axis=0, tiled=True)
    grad_head = lax.dot_general(
        gathered, delta, (((0,), (0,)), ((), ())), preferred_element_type=F32
    ).astype(BF)
    summed = chip_sum(parts.reshape(64, rows // 64, half), grad_head)
    mine = lax.dynamic_slice_in_dim(summed, core * 8, 8, 0)
    rest = swap(lax.dynamic_slice_in_dim(summed, (1 - core) * 8, 8, 0))
    grad_hidden = jnp.where(
        core == 0, jnp.concatenate([mine, rest], 1), jnp.concatenate([rest, mine], 1)
    )
    return grad_hidden, grad_head


def solution(mesh):
    fine = Mesh(mesh.devices.reshape(2, 4, 4, 2, 2), ("zh", "x", "y", "zl", "core"))
    dp, vocab = ("zh", "x"), ("y", "zl", "core")
    return jax.shard_map(
        per_device,
        mesh=fine,
        in_specs=(P(dp, None), P(None, dp + vocab), P(vocab, dp)),
        out_specs=(P(dp + vocab, None), P(None, dp + vocab)),
        check_vma=False,
    )
```

```python
import functools

import jax
import jax.numpy as jnp
from jax import lax
from jax.experimental import pallas as pl
from jax.experimental.pallas import tpu as pltpu
from jax.sharding import Mesh, PartitionSpec as P

BF = jnp.bfloat16
F32 = jnp.float32
CHIPS = ("zh", "x", "y", "zl")
Z = ("zh", "zl")
VMEM_BYTES = 60 << 20
SMEM = pl.BlockSpec(memory_space=pltpu.SMEM)
VMEM = pl.BlockSpec(memory_space=pltpu.VMEM)
ANY = pl.BlockSpec(memory_space=pl.ANY)


def shift(v, axis, size, step):
    return lax.ppermute(v, axis, [(i, (i + step) % size) for i in range(size)])


def swap(v):
    return shift(v, "core", 2, 1)


def total(v):
    v = v + swap(v)
    for axis in ("x", "y", Z):
        v = v + shift(v, axis, 4, 1) + shift(v, axis, 4, 3) + shift(v, axis, 4, 2)
    return v


def left_kernel(block, *refs):
    refs[-1][...] = block[:, : refs[-1].shape[1]]


def left_columns(block, cols, *after):
    return pl.pallas_call(
        left_kernel,
        name="left_columns",
        in_specs=[VMEM] + [ANY] * len(after),
        out_specs=VMEM,
        out_shape=jax.ShapeDtypeStruct((block.shape[0], cols), BF),
        cost_estimate=pl.CostEstimate(flops=0, bytes_accessed=1 << 20, transcendentals=0),
    )(block, *after)


def scores_kernel(tile, place, hidden, *refs):
    own, other, (weight, teacher_sum, gathered, capped, sums) = refs[:10], refs[10:20], refs[20:25]
    rows_v, weight_v, capped_v, part, row_sem, weight_sem, out_sem, capped_sem = refs[25:]
    rows, half = own[0].shape
    loads = [(hidden, rows_v.at[pl.ds(pl.multiple_of(place[0] * rows, rows), rows), :])]
    for side, blocks in ((place[8], own), (1 - place[8], other)):
        for i, block in enumerate(blocks):
            at = pl.multiple_of(place[i + 1 if i < 7 else i - 2] * rows, rows)
            left = half - block.shape[1] if i > 6 else 0
            left = pl.multiple_of(side * half + left, 128)
            loads.append((block, rows_v.at[pl.ds(at, rows), pl.ds(left, block.shape[1])]))
    loads = [pltpu.make_async_copy(a, b, row_sem.at[i]) for i, (a, b) in enumerate(loads)]
    cols = [slice(n * tile, (n + 1) * tile) for n in range(weight.shape[1] // tile)]
    weights = [
        pltpu.make_async_copy(weight.at[:, c], weight_v.at[:, c], weight_sem.at[n])
        for n, c in enumerate(cols)
    ]
    for c in weights[:1] + loads:
        c.start()
    for c in loads:
        c.wait()
    keeps = [pltpu.make_async_copy(rows_v, gathered, out_sem)]
    part[...] = jnp.zeros_like(part)
    for n, c in enumerate(cols):
        if n + 1 < len(cols):
            weights[n + 1].start()
        weights[n].wait()

        @pl.loop(0, rows_v.shape[0] // 512)
        def _(m):
            at = pl.ds(pl.multiple_of(m * 512, 512), 512)
            raw = jnp.dot(rows_v[at, :], weight_v[:, c], preferred_element_type=F32)
            cap = jnp.tanh(raw / 30.0)
            capped_v[at, c] = cap
            e = jnp.exp(15.0 * cap)
            s = part[at, :]
            for k in range(tile // 128):
                s = s + e[:, k * 128 : (k + 1) * 128]
            part[at, :] = s

        keeps.append(
            pltpu.make_async_copy(capped_v.at[:, c], capped.at[:, c], capped_sem.at[n])
        )
        keeps[-1].start()
        if n == 0:
            keeps[0].start()
    sums[0:1, :] = jnp.sum(part[...].T, axis=0, keepdims=True)
    sums[1:2, :] = teacher_sum[...]
    for c in keeps:
        c.wait()


def scores(place, hidden, own, other, weight, teacher_sum):
    (depth, cols), tile = weight.shape, 256
    rows = 8 * hidden.shape[0]
    return pl.pallas_call(
        functools.partial(scores_kernel, tile),
        name="scores",
        out_shape=(
            jax.ShapeDtypeStruct((rows, depth), BF),
            jax.ShapeDtypeStruct((rows, cols), F32),
            jax.ShapeDtypeStruct((2, rows), F32),
        ),
        in_specs=[SMEM] + [ANY] * 22 + [VMEM],
        out_specs=(ANY, ANY, VMEM),
        scratch_shapes=[
            pltpu.VMEM((rows, depth), BF),
            pltpu.VMEM((depth, cols), BF),
            pltpu.VMEM((rows, cols), F32),
            pltpu.VMEM((rows, 128), F32),
            pltpu.SemaphoreType.DMA((21,)),
            pltpu.SemaphoreType.DMA((cols // tile,)),
            pltpu.SemaphoreType.DMA,
            pltpu.SemaphoreType.DMA((cols // tile,)),
        ],
        compiler_params=pltpu.CompilerParams(vmem_limit_bytes=VMEM_BYTES),
        cost_estimate=pl.CostEstimate(
            flops=2 * rows * depth * cols, bytes_accessed=20 << 20, transcendentals=2 * rows * cols
        ),
    )(place, hidden, *own, *other, weight, teacher_sum)


def delta_kernel(core, capped, teacher, totals, weight, delta, share):
    scale = (8192.0 / totals[...]).T
    cap = capped[...]
    student = jnp.exp(15.0 * cap) * scale[:, 0:1]
    target = jnp.exp(teacher[...].astype(F32) * 0.5) * scale[:, 1:2]
    d = ((student - target) * (1.0 - cap * cap)).astype(BF)
    delta[...] = d
    share[...] = lax.dot_general(
        d, weight[...], (((1,), (1,)), ((), ())), preferred_element_type=F32
    ).astype(BF)


def delta_and_share(core, capped, teacher, totals, weight):
    (rows, cols), half, tile = capped.shape, weight.shape[0] // 2, 256
    block = lambda shape, f: pl.BlockSpec(shape, f)
    return pl.pallas_call(
        delta_kernel,
        name="delta_and_share",
        grid_spec=pltpu.PrefetchScalarGridSpec(
            num_scalar_prefetch=1,
            grid=(rows // tile,),
            in_specs=[
                block((tile, cols), lambda i, core: (i, 0)),
                block((tile, cols), lambda i, core: (i, 0)),
                block((8, tile), lambda i, core: (0, i)),
                block((half, cols), lambda i, core: (1 - core[0], 0)),
            ],
            out_specs=[
                block((tile, cols), lambda i, core: (i, 0)),
                block((tile, half), lambda i, core: (i, 0)),
            ],
        ),
        out_shape=(
            jax.ShapeDtypeStruct((rows, cols), BF),
            jax.ShapeDtypeStruct((rows, half), BF),
        ),
        compiler_params=pltpu.CompilerParams(vmem_limit_bytes=40 << 20),
        cost_estimate=pl.CostEstimate(
            flops=2 * rows * half * cols, bytes_accessed=16 << 20, transcendentals=2 * rows * cols
        ),
    )(core, capped, teacher, totals, weight)


def share_kernel(core, delta, weight, share):
    share[...] = lax.dot_general(
        delta[...], weight[...], (((1,), (1,)), ((), ())), preferred_element_type=F32
    ).astype(BF)


def own_share(core, delta, weight):
    (rows, cols), half, tile = delta.shape, weight.shape[0] // 2, 256
    return pl.pallas_call(
        share_kernel,
        name="own_share",
        grid_spec=pltpu.PrefetchScalarGridSpec(
            num_scalar_prefetch=1,
            grid=(rows // tile,),
            in_specs=[
                pl.BlockSpec((tile, cols), lambda i, core: (i, 0)),
                pl.BlockSpec((half, cols), lambda i, core: (core[0], 0)),
            ],
            out_specs=pl.BlockSpec((tile, half), lambda i, core: (i, 0)),
        ),
        out_shape=jax.ShapeDtypeStruct((rows, half), BF),
        compiler_params=pltpu.CompilerParams(vmem_limit_bytes=40 << 20),
        cost_estimate=pl.CostEstimate(
            flops=2 * rows * half * cols, bytes_accessed=10 << 20, transcendentals=0
        ),
    )(core, delta, weight)


def chip_sum_kernel(core, parts, after, mine, rest, total):
    i = pl.program_id(0)
    now = jnp.sum(parts[...].astype(F32), axis=0)

    @pl.when(i == 0)
    def _():
        total[...] = now

    @pl.when(i > 0)
    def _():
        total[...] += now

    @pl.when(i == pl.num_programs(0) - 1)
    def _():
        low, high = total[:8, :], total[8:, :]
        mine[...] = jnp.where(core[0] == 0, low, high).astype(BF)
        rest[...] = jnp.where(core[0] == 0, high, low).astype(BF)


def chip_sum(core, parts, after):
    count, rows, cols = parts.shape
    out = pl.BlockSpec((rows // 2, cols), lambda i: (0, 0))
    return pl.pallas_call(
        chip_sum_kernel,
        name="chip_sum",
        grid=(4,),
        in_specs=[SMEM, pl.BlockSpec((count // 4, rows, cols), lambda i: (i, 0, 0)), ANY],
        out_specs=(out, out),
        out_shape=[jax.ShapeDtypeStruct((rows // 2, cols), BF)] * 2,
        scratch_shapes=[pltpu.VMEM((rows, cols), F32)],
        compiler_params=pltpu.CompilerParams(vmem_limit_bytes=16 << 20),
        cost_estimate=pl.CostEstimate(flops=parts.size, bytes_accessed=4 << 20, transcendentals=0),
    )(core, parts, after)


def per_device(hidden, head_weight, teacher_logits):
    core = lax.axis_index("core")
    zh, x = lax.axis_index("zh"), lax.axis_index("x")
    vocab = lax.axis_index(("y", "zl", "core"))
    half = hidden.shape[1] // 2
    rows = 8 * hidden.shape[0]
    steps = (1, 3, 2)

    group = teacher_logits.shape[0]
    mine = jnp.sum(jnp.exp(teacher_logits.astype(F32) / 2.0), axis=1)
    teacher_sum = lax.dynamic_update_slice_in_dim(
        jnp.zeros((rows,), F32), mine, vocab * group, 0
    )
    by_owner = teacher_logits.reshape(group, 16, -1).transpose(1, 0, 2)
    teacher = lax.all_to_all(
        by_owner, ("y", "zl", "core"), split_axis=0, concat_axis=0, tiled=True
    ).reshape(rows, -1)

    cut = 768
    near = lax.dynamic_slice_in_dim(hidden, core * half, half, 1)
    far = shift(near, "zh", 2, 1)
    left = left_columns(far, cut, mine, by_owner)
    near = [shift(near, "x", 4, s) for s in steps]
    own = near + [far] + [shift(left, "x", 4, s) for s in steps]
    own += [shift(b[:, cut:], "zh", 2, 1) for b in near]
    other = [swap(b) for b in own]
    place = [zh * 4 + (x - s) % 4 for s in (0,) + steps]
    place += [(1 - zh) * 4 + (x - s) % 4 for s in (0,) + steps]
    place = jnp.stack(place + [core]).astype(jnp.int32)

    gathered, capped, sums = scores(place, hidden, own, other, head_weight, teacher_sum[None])
    totals = jnp.concatenate([total(sums), jnp.ones((6, rows), F32)])

    which = core[None].astype(jnp.int32)
    delta, give = delta_and_share(which, capped, teacher, totals, head_weight)
    keep = own_share(which, delta, head_weight)
    chip = (keep.astype(F32) + swap(give).astype(F32)).astype(BF)
    parts = lax.all_to_all(chip, CHIPS, split_axis=0, concat_axis=0, tiled=True)
    grad_head = lax.dot_general(
        gathered, delta, (((0,), (0,)), ((), ())), preferred_element_type=F32
    ).astype(BF)
    mine, rest = chip_sum(which, parts.reshape(64, rows // 64, half), grad_head[:8, :128])
    rest = swap(rest)
    grad_hidden = jnp.where(
        core == 0, jnp.concatenate([mine, rest], 1), jnp.concatenate([rest, mine], 1)
    )
    return grad_hidden, grad_head


def solution(mesh):
    fine = Mesh(mesh.devices.reshape(2, 4, 4, 2, 2), ("zh", "x", "y", "zl", "core"))
    dp, vocab = ("zh", "x"), ("y", "zl", "core")
    return jax.shard_map(
        per_device,
        mesh=fine,
        in_specs=(P(dp, None), P(None, dp + vocab), P(vocab, dp)),
        out_specs=(P(dp + vocab, None), P(None, dp + vocab)),
        check_vma=False,
    )
```

```python
import functools

import jax
import jax.numpy as jnp
from jax import lax
from jax.experimental import pallas as pl
from jax.experimental.pallas import tpu as pltpu
from jax.sharding import Mesh, PartitionSpec as P

BF = jnp.bfloat16
F32 = jnp.float32
EVERY = ("zh", "x", "y", "zl", "core")
Z = ("zh", "zl")
VMEM_BYTES = 60 << 20
SMEM = pl.BlockSpec(memory_space=pltpu.SMEM)
VMEM = pl.BlockSpec(memory_space=pltpu.VMEM)
ANY = pl.BlockSpec(memory_space=pl.ANY)


def shift(v, axis, size, step):
    return lax.ppermute(v, axis, [(i, (i + step) % size) for i in range(size)])


def swap(v):
    return shift(v, "core", 2, 1)


def total(v):
    v = v + swap(v)
    for axis in ("x", "y", Z):
        v = v + shift(v, axis, 4, 1) + shift(v, axis, 4, 3) + shift(v, axis, 4, 2)
    return v


def left_kernel(block, *refs):
    refs[-1][...] = block[:, : refs[-1].shape[1]]


def left_columns(block, cols, *after):
    return pl.pallas_call(
        left_kernel,
        name="left_columns",
        in_specs=[VMEM] + [ANY] * len(after),
        out_specs=VMEM,
        out_shape=jax.ShapeDtypeStruct((block.shape[0], cols), BF),
        cost_estimate=pl.CostEstimate(flops=0, bytes_accessed=1 << 20, transcendentals=0),
    )(block, *after)


def scores_kernel(tile, place, hidden, *refs):
    own, other, (weight, teacher_sum, gathered, capped, sums) = refs[:10], refs[10:20], refs[20:25]
    rows_v, weight_v, capped_v, part, row_sem, weight_sem, out_sem, capped_sem = refs[25:]
    rows, half = own[0].shape
    loads = [(hidden, rows_v.at[pl.ds(pl.multiple_of(place[0] * rows, rows), rows), :])]
    for side, blocks in ((place[8], own), (1 - place[8], other)):
        for i, block in enumerate(blocks):
            at = pl.multiple_of(place[i + 1 if i < 7 else i - 2] * rows, rows)
            left = half - block.shape[1] if i > 6 else 0
            left = pl.multiple_of(side * half + left, 128)
            loads.append((block, rows_v.at[pl.ds(at, rows), pl.ds(left, block.shape[1])]))
    loads = [pltpu.make_async_copy(a, b, row_sem.at[i]) for i, (a, b) in enumerate(loads)]
    cols = [slice(n * tile, (n + 1) * tile) for n in range(weight.shape[1] // tile)]
    weights = [
        pltpu.make_async_copy(weight.at[:, c], weight_v.at[:, c], weight_sem.at[n])
        for n, c in enumerate(cols)
    ]
    for c in weights[:1] + loads:
        c.start()
    for c in loads:
        c.wait()
    keeps = [pltpu.make_async_copy(rows_v, gathered, out_sem)]
    part[...] = jnp.zeros_like(part)
    for n, c in enumerate(cols):
        if n + 1 < len(cols):
            weights[n + 1].start()
        weights[n].wait()

        @pl.loop(0, rows_v.shape[0] // 512)
        def _(m):
            at = pl.ds(pl.multiple_of(m * 512, 512), 512)
            raw = jnp.dot(rows_v[at, :], weight_v[:, c], preferred_element_type=F32)
            cap = jnp.tanh(raw / 30.0)
            capped_v[at, c] = cap
            e = jnp.exp(15.0 * cap)
            s = part[at, :]
            for k in range(tile // 128):
                s = s + e[:, k * 128 : (k + 1) * 128]
            part[at, :] = s

        keeps.append(
            pltpu.make_async_copy(capped_v.at[:, c], capped.at[:, c], capped_sem.at[n])
        )
        keeps[-1].start()
        if n == 0:
            keeps[0].start()
    sums[0:1, :] = jnp.sum(part[...].T, axis=0, keepdims=True)
    sums[1:2, :] = teacher_sum[...]
    for c in keeps:
        c.wait()


def scores(place, hidden, own, other, weight, teacher_sum):
    (depth, cols), tile = weight.shape, 256
    rows = 8 * hidden.shape[0]
    return pl.pallas_call(
        functools.partial(scores_kernel, tile),
        name="scores",
        out_shape=(
            jax.ShapeDtypeStruct((rows, depth), BF),
            jax.ShapeDtypeStruct((rows, cols), F32),
            jax.ShapeDtypeStruct((2, rows), F32),
        ),
        in_specs=[SMEM] + [ANY] * 22 + [VMEM],
        out_specs=(ANY, ANY, VMEM),
        scratch_shapes=[
            pltpu.VMEM((rows, depth), BF),
            pltpu.VMEM((depth, cols), BF),
            pltpu.VMEM((rows, cols), F32),
            pltpu.VMEM((rows, 128), F32),
            pltpu.SemaphoreType.DMA((21,)),
            pltpu.SemaphoreType.DMA((cols // tile,)),
            pltpu.SemaphoreType.DMA,
            pltpu.SemaphoreType.DMA((cols // tile,)),
        ],
        compiler_params=pltpu.CompilerParams(vmem_limit_bytes=VMEM_BYTES),
        cost_estimate=pl.CostEstimate(
            flops=2 * rows * depth * cols, bytes_accessed=20 << 20, transcendentals=2 * rows * cols
        ),
    )(place, hidden, *own, *other, weight, teacher_sum)


def delta_kernel(core, capped, teacher, totals, weight, delta, share):
    scale = (8192.0 / totals[...]).T
    cap = capped[...]
    student = jnp.exp(15.0 * cap) * scale[:, 0:1]
    target = jnp.exp(teacher[...].astype(F32) * 0.5) * scale[:, 1:2]
    d = ((student - target) * (1.0 - cap * cap)).astype(BF)
    delta[...] = d
    share[...] = lax.dot_general(
        d, weight[...], (((1,), (1,)), ((), ())), preferred_element_type=F32
    ).astype(BF)


def delta_and_share(core, capped, teacher, totals, weight):
    (rows, cols), half, tile = capped.shape, weight.shape[0] // 2, 256
    block = lambda shape, f: pl.BlockSpec(shape, f)
    return pl.pallas_call(
        delta_kernel,
        name="delta_and_share",
        grid_spec=pltpu.PrefetchScalarGridSpec(
            num_scalar_prefetch=1,
            grid=(rows // tile,),
            in_specs=[
                block((tile, cols), lambda i, core: (i, 0)),
                block((tile, cols), lambda i, core: (i, 0)),
                block((8, tile), lambda i, core: (0, i)),
                block((half, cols), lambda i, core: (1 - core[0], 0)),
            ],
            out_specs=[
                block((tile, cols), lambda i, core: (i, 0)),
                block((tile, half), lambda i, core: (i, 0)),
            ],
        ),
        out_shape=(
            jax.ShapeDtypeStruct((rows, cols), BF),
            jax.ShapeDtypeStruct((rows, half), BF),
        ),
        compiler_params=pltpu.CompilerParams(vmem_limit_bytes=40 << 20),
        cost_estimate=pl.CostEstimate(
            flops=2 * rows * half * cols, bytes_accessed=16 << 20, transcendentals=2 * rows * cols
        ),
    )(core, capped, teacher, totals, weight)


def share_kernel(core, delta, weight, share, weight_v, sem):
    half = weight_v.shape[0]
    at = pl.ds(pl.multiple_of(core[0] * half, half), half)
    load = pltpu.make_async_copy(weight.at[at, :], weight_v, sem)

    @pl.when(pl.program_id(0) == 0)
    def _():
        load.start()
        load.wait()

    share[...] = lax.dot_general(
        delta[...], weight_v[...], (((1,), (1,)), ((), ())), preferred_element_type=F32
    ).astype(BF)


def own_share(core, delta, weight):
    (rows, cols), half, tile = delta.shape, weight.shape[0] // 2, 256
    return pl.pallas_call(
        share_kernel,
        name="own_share",
        grid_spec=pltpu.PrefetchScalarGridSpec(
            num_scalar_prefetch=1,
            grid=(rows // tile,),
            in_specs=[pl.BlockSpec((tile, cols), lambda i, core: (i, 0)), ANY],
            out_specs=pl.BlockSpec((tile, half), lambda i, core: (i, 0)),
            scratch_shapes=[pltpu.VMEM((half, cols), BF), pltpu.SemaphoreType.DMA],
        ),
        out_shape=jax.ShapeDtypeStruct((rows, half), BF),
        compiler_params=pltpu.CompilerParams(vmem_limit_bytes=40 << 20),
        cost_estimate=pl.CostEstimate(
            flops=2 * rows * half * cols, bytes_accessed=10 << 20, transcendentals=0
        ),
    )(core, delta, weight)


def chip_sum_kernel(parts, after, out, total):
    i = pl.program_id(0)
    now = jnp.sum(parts[...].astype(F32), axis=0)

    @pl.when(i == 0)
    def _():
        total[...] = now

    @pl.when(i > 0)
    def _():
        total[...] += now

    @pl.when(i == pl.num_programs(0) - 1)
    def _():
        half = total.shape[2]
        for k in range(2):
            out[:, k * half : (k + 1) * half] = total[k].astype(BF)


def chip_sum(parts, after):
    count, cores, rows, cols = parts.shape
    return pl.pallas_call(
        chip_sum_kernel,
        name="chip_sum",
        grid=(4,),
        in_specs=[
            pl.BlockSpec((count // 4, cores, rows, cols), lambda i: (i, 0, 0, 0)),
            ANY,
        ],
        out_specs=pl.BlockSpec((rows, cores * cols), lambda i: (0, 0)),
        out_shape=jax.ShapeDtypeStruct((rows, cores * cols), BF),
        scratch_shapes=[pltpu.VMEM((cores, rows, cols), F32)],
        compiler_params=pltpu.CompilerParams(vmem_limit_bytes=16 << 20),
        cost_estimate=pl.CostEstimate(flops=parts.size, bytes_accessed=4 << 20, transcendentals=0),
    )(parts, after)


def per_device(hidden, head_weight, teacher_logits):
    core = lax.axis_index("core")
    zh, x = lax.axis_index("zh"), lax.axis_index("x")
    vocab = lax.axis_index(("y", "zl", "core"))
    half = hidden.shape[1] // 2
    rows = 8 * hidden.shape[0]
    steps = (1, 3, 2)

    group = teacher_logits.shape[0]
    mine = jnp.sum(jnp.exp(teacher_logits.astype(F32) / 2.0), axis=1)
    teacher_sum = lax.dynamic_update_slice_in_dim(
        jnp.zeros((rows,), F32), mine, vocab * group, 0
    )
    by_owner = teacher_logits.reshape(group, 16, -1).transpose(1, 0, 2)
    teacher = lax.all_to_all(
        by_owner, ("y", "zl", "core"), split_axis=0, concat_axis=0, tiled=True
    ).reshape(rows, -1)

    cut = 768
    near = lax.dynamic_slice_in_dim(hidden, core * half, half, 1)
    far = shift(near, "zh", 2, 1)
    left = left_columns(far, cut, mine, by_owner)
    near = [shift(near, "x", 4, s) for s in steps]
    own = near + [far] + [shift(left, "x", 4, s) for s in steps]
    own += [shift(b[:, cut:], "zh", 2, 1) for b in near]
    other = [swap(b) for b in own]
    place = [zh * 4 + (x - s) % 4 for s in (0,) + steps]
    place += [(1 - zh) * 4 + (x - s) % 4 for s in (0,) + steps]
    place = jnp.stack(place + [core]).astype(jnp.int32)

    gathered, capped, sums = scores(place, hidden, own, other, head_weight, teacher_sum[None])
    totals = jnp.concatenate([total(sums), jnp.ones((6, rows), F32)])

    which = core[None].astype(jnp.int32)
    delta, give = delta_and_share(which, capped, teacher, totals, head_weight)
    keep = own_share(which, delta, head_weight)
    chip = (keep.astype(F32) + swap(give).astype(F32)).astype(BF)
    parts = lax.all_to_all(
        chip.reshape(128, rows // 128, half), EVERY, split_axis=0, concat_axis=0, tiled=True
    )
    grad_head = lax.dot_general(
        gathered, delta, (((0,), (0,)), ((), ())), preferred_element_type=F32
    ).astype(BF)
    grad_hidden = chip_sum(parts.reshape(64, 2, rows // 128, half), grad_head[:8, :128])
    return grad_hidden, grad_head


def solution(mesh):
    fine = Mesh(mesh.devices.reshape(2, 4, 4, 2, 2), ("zh", "x", "y", "zl", "core"))
    dp, vocab = ("zh", "x"), ("y", "zl", "core")
    return jax.shard_map(
        per_device,
        mesh=fine,
        in_specs=(P(dp, None), P(None, dp + vocab), P(vocab, dp)),
        out_specs=(P(dp + vocab, None), P(None, dp + vocab)),
        check_vma=False,
    )
```

```python
import functools

import jax
import jax.numpy as jnp
from jax import lax
from jax.experimental import pallas as pl
from jax.experimental.pallas import tpu as pltpu
from jax.sharding import Mesh, PartitionSpec as P

BF = jnp.bfloat16
F32 = jnp.float32
EVERY = ("zh", "x", "y", "zl", "core")
Z = ("zh", "zl")
VMEM_BYTES = 60 << 20
SMEM = pl.BlockSpec(memory_space=pltpu.SMEM)
VMEM = pl.BlockSpec(memory_space=pltpu.VMEM)
ANY = pl.BlockSpec(memory_space=pl.ANY)


def shift(v, axis, size, step):
    return lax.ppermute(v, axis, [(i, (i + step) % size) for i in range(size)])


def swap(v):
    return shift(v, "core", 2, 1)


def total(v):
    v = v + swap(v)
    for axis in ("x", "y", Z):
        v = v + shift(v, axis, 4, 1) + shift(v, axis, 4, 3) + shift(v, axis, 4, 2)
    return v


def left_kernel(block, *refs):
    refs[-1][...] = block[:, : refs[-1].shape[1]]


def left_columns(block, cols, *after):
    return pl.pallas_call(
        left_kernel,
        name="left_columns",
        in_specs=[VMEM] + [ANY] * len(after),
        out_specs=VMEM,
        out_shape=jax.ShapeDtypeStruct((block.shape[0], cols), BF),
        cost_estimate=pl.CostEstimate(flops=0, bytes_accessed=1 << 20, transcendentals=0),
    )(block, *after)


def scores_kernel(tile, place, hidden, *refs):
    own, other, (weight, teacher_sum, gathered, capped, sums) = refs[:10], refs[10:20], refs[20:25]
    rows_v, weight_v, capped_v, part, row_sem, weight_sem, out_sem, capped_sem = refs[25:]
    rows, half = own[0].shape
    loads = [(hidden, rows_v.at[pl.ds(pl.multiple_of(place[0] * rows, rows), rows), :])]
    for side, blocks in ((place[8], own), (1 - place[8], other)):
        for i, block in enumerate(blocks):
            at = pl.multiple_of(place[i + 1 if i < 7 else i - 2] * rows, rows)
            left = half - block.shape[1] if i > 6 else 0
            left = pl.multiple_of(side * half + left, 128)
            loads.append((block, rows_v.at[pl.ds(at, rows), pl.ds(left, block.shape[1])]))
    loads = [pltpu.make_async_copy(a, b, row_sem.at[i]) for i, (a, b) in enumerate(loads)]
    cols = [slice(n * tile, (n + 1) * tile) for n in range(weight.shape[1] // tile)]
    weights = [
        pltpu.make_async_copy(weight.at[:, c], weight_v.at[:, c], weight_sem.at[n])
        for n, c in enumerate(cols)
    ]
    for c in weights[:1] + loads:
        c.start()
    for c in loads:
        c.wait()
    keeps = [pltpu.make_async_copy(rows_v, gathered, out_sem)]
    part[...] = jnp.zeros_like(part)
    for n, c in enumerate(cols):
        if n + 1 < len(cols):
            weights[n + 1].start()
        weights[n].wait()

        @pl.loop(0, rows_v.shape[0] // 512)
        def _(m):
            at = pl.ds(pl.multiple_of(m * 512, 512), 512)
            raw = jnp.dot(rows_v[at, :], weight_v[:, c], preferred_element_type=F32)
            cap = jnp.tanh(raw / 30.0)
            capped_v[at, c] = cap
            e = jnp.exp(15.0 * cap)
            s = part[at, :]
            for k in range(tile // 128):
                s = s + e[:, k * 128 : (k + 1) * 128]
            part[at, :] = s

        keeps.append(
            pltpu.make_async_copy(capped_v.at[:, c], capped.at[:, c], capped_sem.at[n])
        )
        keeps[-1].start()
        if n == 0:
            keeps[0].start()
    sums[0:1, :] = jnp.sum(part[...].T, axis=0, keepdims=True)
    sums[1:2, :] = teacher_sum[...]
    for c in keeps:
        c.wait()


def scores(place, hidden, own, other, weight, teacher_sum):
    (depth, cols), tile = weight.shape, 256
    rows = 8 * hidden.shape[0]
    return pl.pallas_call(
        functools.partial(scores_kernel, tile),
        name="scores",
        out_shape=(
            jax.ShapeDtypeStruct((rows, depth), BF),
            jax.ShapeDtypeStruct((rows, cols), F32),
            jax.ShapeDtypeStruct((2, rows), F32),
        ),
        in_specs=[SMEM] + [ANY] * 22 + [VMEM],
        out_specs=(ANY, ANY, VMEM),
        scratch_shapes=[
            pltpu.VMEM((rows, depth), BF),
            pltpu.VMEM((depth, cols), BF),
            pltpu.VMEM((rows, cols), F32),
            pltpu.VMEM((rows, 128), F32),
            pltpu.SemaphoreType.DMA((21,)),
            pltpu.SemaphoreType.DMA((cols // tile,)),
            pltpu.SemaphoreType.DMA,
            pltpu.SemaphoreType.DMA((cols // tile,)),
        ],
        compiler_params=pltpu.CompilerParams(vmem_limit_bytes=VMEM_BYTES),
        cost_estimate=pl.CostEstimate(
            flops=2 * rows * depth * cols, bytes_accessed=20 << 20, transcendentals=2 * rows * cols
        ),
    )(place, hidden, *own, *other, weight, teacher_sum)


def delta_kernel(core, capped, teacher, totals, weight, delta, share, own, weight_v, sem):
    half = weight_v.shape[0]
    at = pl.ds(pl.multiple_of((1 - core[0]) * half, half), half)
    load = pltpu.make_async_copy(weight.at[at, :], weight_v, sem.at[0])
    at = pl.ds(pl.multiple_of(core[0] * half, half), half)
    ahead = pltpu.make_async_copy(weight.at[at, :], own, sem.at[1])
    i = pl.program_id(0)

    @pl.when(i == 0)
    def _():
        load.start()
        ahead.start()

    scale = (8192.0 / totals[...]).T
    cap = capped[...]
    student = jnp.exp(15.0 * cap) * scale[:, 0:1]
    target = jnp.exp(teacher[...].astype(F32) * 0.5) * scale[:, 1:2]
    d = ((student - target) * (1.0 - cap * cap)).astype(BF)
    delta[...] = d

    @pl.when(i == 0)
    def _():
        load.wait()

    share[...] = lax.dot_general(
        d, weight_v[...], (((1,), (1,)), ((), ())), preferred_element_type=F32
    ).astype(BF)

    @pl.when(i == pl.num_programs(0) - 1)
    def _():
        ahead.wait()


def delta_and_share(core, capped, teacher, totals, weight):
    (rows, cols), half, tile = capped.shape, weight.shape[0] // 2, 256
    block = lambda shape, f: pl.BlockSpec(shape, f)
    return pl.pallas_call(
        delta_kernel,
        name="delta_and_share",
        grid_spec=pltpu.PrefetchScalarGridSpec(
            num_scalar_prefetch=1,
            grid=(rows // tile,),
            in_specs=[
                block((tile, cols), lambda i, core: (i, 0)),
                block((tile, cols), lambda i, core: (i, 0)),
                block((8, tile), lambda i, core: (0, i)),
                ANY,
            ],
            out_specs=[
                block((tile, cols), lambda i, core: (i, 0)),
                block((tile, half), lambda i, core: (i, 0)),
                ANY,
            ],
            scratch_shapes=[pltpu.VMEM((half, cols), BF), pltpu.SemaphoreType.DMA((2,))],
        ),
        out_shape=(
            jax.ShapeDtypeStruct((rows, cols), BF),
            jax.ShapeDtypeStruct((rows, half), BF),
            pltpu.VMEM((half, cols), BF),
        ),
        compiler_params=pltpu.CompilerParams(vmem_limit_bytes=36 << 20),
        cost_estimate=pl.CostEstimate(
            flops=2 * rows * half * cols, bytes_accessed=16 << 20, transcendentals=2 * rows * cols
        ),
    )(core, capped, teacher, totals, weight)


def share_kernel(delta, weight, share):
    share[...] = lax.dot_general(
        delta[...], weight[...], (((1,), (1,)), ((), ())), preferred_element_type=F32
    ).astype(BF)


def own_share(delta, weight):
    (rows, cols), half, tile = delta.shape, weight.shape[0], 256
    return pl.pallas_call(
        share_kernel,
        name="own_share",
        grid=(rows // tile,),
        in_specs=[pl.BlockSpec((tile, cols), lambda i: (i, 0)), VMEM],
        out_specs=pl.BlockSpec((tile, half), lambda i: (i, 0)),
        out_shape=jax.ShapeDtypeStruct((rows, half), BF),
        compiler_params=pltpu.CompilerParams(vmem_limit_bytes=36 << 20),
        cost_estimate=pl.CostEstimate(
            flops=2 * rows * half * cols, bytes_accessed=10 << 20, transcendentals=0
        ),
    )(delta, weight)


def chip_sum_kernel(parts, after, out, total):
    i = pl.program_id(0)
    now = jnp.sum(parts[...].astype(F32), axis=0)

    @pl.when(i == 0)
    def _():
        total[...] = now

    @pl.when(i > 0)
    def _():
        total[...] += now

    @pl.when(i == pl.num_programs(0) - 1)
    def _():
        half = total.shape[2]
        for k in range(2):
            out[:, k * half : (k + 1) * half] = total[k].astype(BF)


def chip_sum(parts, after):
    count, cores, rows, cols = parts.shape
    return pl.pallas_call(
        chip_sum_kernel,
        name="chip_sum",
        grid=(4,),
        in_specs=[
            pl.BlockSpec((count // 4, cores, rows, cols), lambda i: (i, 0, 0, 0)),
            ANY,
        ],
        out_specs=pl.BlockSpec((rows, cores * cols), lambda i: (0, 0)),
        out_shape=jax.ShapeDtypeStruct((rows, cores * cols), BF),
        scratch_shapes=[pltpu.VMEM((cores, rows, cols), F32)],
        compiler_params=pltpu.CompilerParams(vmem_limit_bytes=16 << 20),
        cost_estimate=pl.CostEstimate(flops=parts.size, bytes_accessed=4 << 20, transcendentals=0),
    )(parts, after)


def per_device(hidden, head_weight, teacher_logits):
    core = lax.axis_index("core")
    zh, x = lax.axis_index("zh"), lax.axis_index("x")
    vocab = lax.axis_index(("y", "zl", "core"))
    half = hidden.shape[1] // 2
    rows = 8 * hidden.shape[0]
    steps = (1, 3, 2)

    group = teacher_logits.shape[0]
    mine = jnp.sum(jnp.exp(teacher_logits.astype(F32) / 2.0), axis=1)
    teacher_sum = lax.dynamic_update_slice_in_dim(
        jnp.zeros((rows,), F32), mine, vocab * group, 0
    )
    by_owner = teacher_logits.reshape(group, 16, -1).transpose(1, 0, 2)
    teacher = lax.all_to_all(
        by_owner, ("y", "zl", "core"), split_axis=0, concat_axis=0, tiled=True
    ).reshape(rows, -1)

    cut = 768
    near = lax.dynamic_slice_in_dim(hidden, core * half, half, 1)
    far = shift(near, "zh", 2, 1)
    left = left_columns(far, cut, mine, by_owner)
    near = [shift(near, "x", 4, s) for s in steps]
    own = near + [far] + [shift(left, "x", 4, s) for s in steps]
    own += [shift(b[:, cut:], "zh", 2, 1) for b in near]
    other = [swap(b) for b in own]
    place = [zh * 4 + (x - s) % 4 for s in (0,) + steps]
    place += [(1 - zh) * 4 + (x - s) % 4 for s in (0,) + steps]
    place = jnp.stack(place + [core]).astype(jnp.int32)

    gathered, capped, sums = scores(place, hidden, own, other, head_weight, teacher_sum[None])
    totals = jnp.concatenate([total(sums), jnp.ones((6, rows), F32)])

    which = core[None].astype(jnp.int32)
    delta, give, own_weight = delta_and_share(which, capped, teacher, totals, head_weight)
    keep = own_share(delta, own_weight)
    chip = (keep.astype(F32) + swap(give).astype(F32)).astype(BF)
    parts = lax.all_to_all(
        chip.reshape(128, rows // 128, half), EVERY, split_axis=0, concat_axis=0, tiled=True
    )
    grad_head = lax.dot_general(
        gathered, delta, (((0,), (0,)), ((), ())), preferred_element_type=F32
    ).astype(BF)
    grad_hidden = chip_sum(parts.reshape(64, 2, rows // 128, half), grad_head[:8, :128])
    return grad_hidden, grad_head


def solution(mesh):
    fine = Mesh(mesh.devices.reshape(2, 4, 4, 2, 2), ("zh", "x", "y", "zl", "core"))
    dp, vocab = ("zh", "x"), ("y", "zl", "core")
    return jax.shard_map(
        per_device,
        mesh=fine,
        in_specs=(P(dp, None), P(None, dp + vocab), P(vocab, dp)),
        out_specs=(P(dp + vocab, None), P(None, dp + vocab)),
        check_vma=False,
    )
```

```python
import functools
import math

import jax
import jax.numpy as jnp
from jax import lax
from jax.experimental import pallas as pl
from jax.experimental.pallas import tpu as pltpu
from jax.sharding import Mesh, PartitionSpec as P

BF = jnp.bfloat16
F32 = jnp.float32
EVERY = ("zh", "x", "y", "zl", "core")
Z = ("zh", "zl")
VMEM_BYTES = 60 << 20
EXPONENT = 15.0 * math.log2(math.e)
SMEM = pl.BlockSpec(memory_space=pltpu.SMEM)
VMEM = pl.BlockSpec(memory_space=pltpu.VMEM)
ANY = pl.BlockSpec(memory_space=pl.ANY)


def shift(v, axis, size, step):
    return lax.ppermute(v, axis, [(i, (i + step) % size) for i in range(size)])


def swap(v):
    return shift(v, "core", 2, 1)


def total(v):
    v = v + swap(v)
    for axis in ("x", "y", Z):
        v = v + shift(v, axis, 4, 1) + shift(v, axis, 4, 3) + shift(v, axis, 4, 2)
    return v


def left_kernel(block, *refs):
    refs[-1][...] = block[:, : refs[-1].shape[1]]


def left_columns(block, cols, *after):
    return pl.pallas_call(
        left_kernel,
        name="left_columns",
        in_specs=[VMEM] + [ANY] * len(after),
        out_specs=VMEM,
        out_shape=jax.ShapeDtypeStruct((block.shape[0], cols), BF),
        cost_estimate=pl.CostEstimate(flops=0, bytes_accessed=1 << 20, transcendentals=0),
    )(block, *after)


def scores_kernel(tile, place, hidden, *refs):
    own, other, (weight, teacher_sum, gathered, capped, sums) = refs[:10], refs[10:20], refs[20:25]
    rows_v, weight_v, capped_v, part, row_sem, weight_sem, out_sem, capped_sem = refs[25:]
    rows, half = own[0].shape
    loads = [(hidden, rows_v.at[pl.ds(pl.multiple_of(place[0] * rows, rows), rows), :])]
    for side, blocks in ((place[8], own), (1 - place[8], other)):
        for i, block in enumerate(blocks):
            at = pl.multiple_of(place[i + 1 if i < 7 else i - 2] * rows, rows)
            left = half - block.shape[1] if i > 6 else 0
            left = pl.multiple_of(side * half + left, 128)
            loads.append((block, rows_v.at[pl.ds(at, rows), pl.ds(left, block.shape[1])]))
    loads = [pltpu.make_async_copy(a, b, row_sem.at[i]) for i, (a, b) in enumerate(loads)]
    cols = [slice(n * tile, (n + 1) * tile) for n in range(weight.shape[1] // tile)]
    weights = [
        pltpu.make_async_copy(weight.at[:, c], weight_v.at[:, c], weight_sem.at[n])
        for n, c in enumerate(cols)
    ]
    for c in weights[:1] + loads:
        c.start()
    for c in loads:
        c.wait()
    keeps = [pltpu.make_async_copy(rows_v, gathered, out_sem)]
    part[...] = jnp.zeros_like(part)
    for n, c in enumerate(cols):
        if n + 1 < len(cols):
            weights[n + 1].start()
        weights[n].wait()

        @pl.loop(0, rows_v.shape[0] // 512)
        def _(m):
            at = pl.ds(pl.multiple_of(m * 512, 512), 512)
            raw = jnp.dot(rows_v[at, :], weight_v[:, c], preferred_element_type=F32)
            cap = jnp.tanh(raw * (1.0 / 30.0))
            capped_v[at, c] = cap
            e = jnp.exp2(EXPONENT * cap)
            s = part[at, :]
            for k in range(tile // 128):
                s = s + e[:, k * 128 : (k + 1) * 128]
            part[at, :] = s

        keeps.append(
            pltpu.make_async_copy(capped_v.at[:, c], capped.at[:, c], capped_sem.at[n])
        )
        keeps[-1].start()
        if n == 0:
            keeps[0].start()
    sums[0:1, :] = jnp.sum(part[...].T, axis=0, keepdims=True)
    sums[1:2, :] = teacher_sum[...]
    for c in keeps:
        c.wait()


def scores(place, hidden, own, other, weight, teacher_sum):
    (depth, cols), tile = weight.shape, 256
    rows = 8 * hidden.shape[0]
    return pl.pallas_call(
        functools.partial(scores_kernel, tile),
        name="scores",
        out_shape=(
            jax.ShapeDtypeStruct((rows, depth), BF),
            jax.ShapeDtypeStruct((rows, cols), F32),
            jax.ShapeDtypeStruct((2, rows), F32),
        ),
        in_specs=[SMEM] + [ANY] * 22 + [VMEM],
        out_specs=(ANY, ANY, VMEM),
        scratch_shapes=[
            pltpu.VMEM((rows, depth), BF),
            pltpu.VMEM((depth, cols), BF),
            pltpu.VMEM((rows, cols), F32),
            pltpu.VMEM((rows, 128), F32),
            pltpu.SemaphoreType.DMA((21,)),
            pltpu.SemaphoreType.DMA((cols // tile,)),
            pltpu.SemaphoreType.DMA,
            pltpu.SemaphoreType.DMA((cols // tile,)),
        ],
        compiler_params=pltpu.CompilerParams(vmem_limit_bytes=VMEM_BYTES),
        cost_estimate=pl.CostEstimate(
            flops=2 * rows * depth * cols, bytes_accessed=20 << 20, transcendentals=2 * rows * cols
        ),
    )(place, hidden, *own, *other, weight, teacher_sum)


def delta_kernel(core, capped, teacher, totals, weight, delta, share, own, weight_v, sem):
    half = weight_v.shape[0]
    at = pl.ds(pl.multiple_of((1 - core[0]) * half, half), half)
    load = pltpu.make_async_copy(weight.at[at, :], weight_v, sem.at[0])
    at = pl.ds(pl.multiple_of(core[0] * half, half), half)
    ahead = pltpu.make_async_copy(weight.at[at, :], own, sem.at[1])
    i = pl.program_id(0)

    @pl.when(i == 0)
    def _():
        load.start()
        ahead.start()

    scale = (8192.0 / totals[...]).T
    cap = capped[...]
    student = jnp.exp2(EXPONENT * cap) * scale[:, 0:1]
    target = jnp.exp2(teacher[...].astype(F32) * (EXPONENT / 30.0)) * scale[:, 1:2]
    d = ((student - target) * (1.0 - cap * cap)).astype(BF)
    delta[...] = d

    @pl.when(i == 0)
    def _():
        load.wait()

    share[...] = lax.dot_general(
        d, weight_v[...], (((1,), (1,)), ((), ())), preferred_element_type=F32
    ).astype(BF)

    @pl.when(i == pl.num_programs(0) - 1)
    def _():
        ahead.wait()


def delta_and_share(core, capped, teacher, totals, weight):
    (rows, cols), half, tile = capped.shape, weight.shape[0] // 2, 256
    block = lambda shape, f: pl.BlockSpec(shape, f)
    return pl.pallas_call(
        delta_kernel,
        name="delta_and_share",
        grid_spec=pltpu.PrefetchScalarGridSpec(
            num_scalar_prefetch=1,
            grid=(rows // tile,),
            in_specs=[
                block((tile, cols), lambda i, core: (i, 0)),
                block((tile, cols), lambda i, core: (i, 0)),
                block((8, tile), lambda i, core: (0, i)),
                ANY,
            ],
            out_specs=[
                block((tile, cols), lambda i, core: (i, 0)),
                block((tile, half), lambda i, core: (i, 0)),
                ANY,
            ],
            scratch_shapes=[pltpu.VMEM((half, cols), BF), pltpu.SemaphoreType.DMA((2,))],
        ),
        out_shape=(
            jax.ShapeDtypeStruct((rows, cols), BF),
            jax.ShapeDtypeStruct((rows, half), BF),
            pltpu.VMEM((half, cols), BF),
        ),
        compiler_params=pltpu.CompilerParams(vmem_limit_bytes=36 << 20),
        cost_estimate=pl.CostEstimate(
            flops=2 * rows * half * cols, bytes_accessed=16 << 20, transcendentals=2 * rows * cols
        ),
    )(core, capped, teacher, totals, weight)


def share_kernel(delta, weight, share):
    share[...] = lax.dot_general(
        delta[...], weight[...], (((1,), (1,)), ((), ())), preferred_element_type=F32
    ).astype(BF)


def own_share(delta, weight):
    (rows, cols), half, tile = delta.shape, weight.shape[0], 256
    return pl.pallas_call(
        share_kernel,
        name="own_share",
        grid=(rows // tile,),
        in_specs=[pl.BlockSpec((tile, cols), lambda i: (i, 0)), VMEM],
        out_specs=pl.BlockSpec((tile, half), lambda i: (i, 0)),
        out_shape=jax.ShapeDtypeStruct((rows, half), BF),
        compiler_params=pltpu.CompilerParams(vmem_limit_bytes=36 << 20),
        cost_estimate=pl.CostEstimate(
            flops=2 * rows * half * cols, bytes_accessed=10 << 20, transcendentals=0
        ),
    )(delta, weight)


def chip_sum_kernel(parts, after, out, parts_v, total, sem):
    count = parts.shape[0] // sem.shape[0]
    pieces = [pl.ds(i * count, count) for i in range(sem.shape[0])]
    loads = [
        pltpu.make_async_copy(parts.at[p], parts_v.at[p], sem.at[i]) for i, p in enumerate(pieces)
    ]
    for c in loads:
        c.start()
    for i, p in enumerate(pieces):
        loads[i].wait()
        now = jnp.sum(parts_v[p].astype(F32), axis=0)
        total[...] = now if i == 0 else total[...] + now
    rows, half = out.shape[0], total.shape[1]
    for k in range(2):
        out[:, k * half : (k + 1) * half] = total[k * rows : (k + 1) * rows, :].astype(BF)


def chip_sum(parts, after):
    count, rows, cols = parts.shape
    return pl.pallas_call(
        chip_sum_kernel,
        name="chip_sum",
        in_specs=[ANY, ANY],
        out_specs=VMEM,
        out_shape=jax.ShapeDtypeStruct((rows // 2, 2 * cols), BF),
        scratch_shapes=[
            pltpu.VMEM((count, rows, cols), BF),
            pltpu.VMEM((rows, cols), F32),
            pltpu.SemaphoreType.DMA((8,)),
        ],
        compiler_params=pltpu.CompilerParams(vmem_limit_bytes=16 << 20),
        cost_estimate=pl.CostEstimate(flops=parts.size, bytes_accessed=4 << 20, transcendentals=0),
    )(parts, after)


def per_device(hidden, head_weight, teacher_logits):
    core = lax.axis_index("core")
    zh, x = lax.axis_index("zh"), lax.axis_index("x")
    vocab = lax.axis_index(("y", "zl", "core"))
    half = hidden.shape[1] // 2
    rows = 8 * hidden.shape[0]
    steps = (1, 3, 2)

    group = teacher_logits.shape[0]
    mine = jnp.sum(jnp.exp(teacher_logits.astype(F32) / 2.0), axis=1)
    teacher_sum = lax.dynamic_update_slice_in_dim(
        jnp.zeros((rows,), F32), mine, vocab * group, 0
    )
    by_owner = teacher_logits.reshape(group, 16, -1).transpose(1, 0, 2)
    teacher = lax.all_to_all(
        by_owner, ("y", "zl", "core"), split_axis=0, concat_axis=0, tiled=True
    ).reshape(rows, -1)

    cut = 768
    near = lax.dynamic_slice_in_dim(hidden, core * half, half, 1)
    far = shift(near, "zh", 2, 1)
    left = left_columns(far, cut, mine, by_owner)
    near = [shift(near, "x", 4, s) for s in steps]
    own = near + [far] + [shift(left, "x", 4, s) for s in steps]
    own += [shift(b[:, cut:], "zh", 2, 1) for b in near]
    other = [swap(b) for b in own]
    place = [zh * 4 + (x - s) % 4 for s in (0,) + steps]
    place += [(1 - zh) * 4 + (x - s) % 4 for s in (0,) + steps]
    place = jnp.stack(place + [core]).astype(jnp.int32)

    gathered, capped, sums = scores(place, hidden, own, other, head_weight, teacher_sum[None])
    totals = jnp.concatenate([total(sums), jnp.ones((6, rows), F32)])

    which = core[None].astype(jnp.int32)
    delta, give, own_weight = delta_and_share(which, capped, teacher, totals, head_weight)
    keep = own_share(delta, own_weight)
    chip = (keep.astype(F32) + swap(give).astype(F32)).astype(BF)
    parts = lax.all_to_all(
        chip.reshape(128, rows // 128, half), EVERY, split_axis=0, concat_axis=0, tiled=True
    )
    grad_head = lax.dot_general(
        gathered, delta, (((0,), (0,)), ((), ())), preferred_element_type=F32
    ).astype(BF)
    grad_hidden = chip_sum(parts.reshape(64, rows // 64, half), grad_head[:8, :128])
    return grad_hidden, grad_head


def solution(mesh):
    fine = Mesh(mesh.devices.reshape(2, 4, 4, 2, 2), ("zh", "x", "y", "zl", "core"))
    dp, vocab = ("zh", "x"), ("y", "zl", "core")
    return jax.shard_map(
        per_device,
        mesh=fine,
        in_specs=(P(dp, None), P(None, dp + vocab), P(vocab, dp)),
        out_specs=(P(dp + vocab, None), P(None, dp + vocab)),
        check_vma=False,
    )
```

```python
import functools
import math

import jax
import jax.numpy as jnp
from jax import lax
from jax.experimental import pallas as pl
from jax.experimental.pallas import tpu as pltpu
from jax.sharding import Mesh, PartitionSpec as P

BF = jnp.bfloat16
F32 = jnp.float32
EVERY = ("zh", "x", "y", "zl", "core")
Z = ("zh", "zl")
VMEM_BYTES = 60 << 20
EXPONENT = 15.0 * math.log2(math.e)
SMEM = pl.BlockSpec(memory_space=pltpu.SMEM)
VMEM = pl.BlockSpec(memory_space=pltpu.VMEM)
ANY = pl.BlockSpec(memory_space=pl.ANY)


def shift(v, axis, size, step):
    return lax.ppermute(v, axis, [(i, (i + step) % size) for i in range(size)])


def swap(v):
    return shift(v, "core", 2, 1)


def total(v):
    v = v + swap(v)
    for axis in ("x", "y", Z):
        v = v + shift(v, axis, 4, 1) + shift(v, axis, 4, 3) + shift(v, axis, 4, 2)
    return v


def left_kernel(block, *refs):
    refs[-1][...] = block[:, : refs[-1].shape[1]]


def left_columns(block, cols, *after):
    return pl.pallas_call(
        left_kernel,
        name="left_columns",
        in_specs=[VMEM] + [ANY] * len(after),
        out_specs=VMEM,
        out_shape=jax.ShapeDtypeStruct((block.shape[0], cols), BF),
        cost_estimate=pl.CostEstimate(flops=0, bytes_accessed=1 << 20, transcendentals=0),
    )(block, *after)


def scores_kernel(tile, place, hidden, *refs):
    own, other, (weight, teacher_sum, gathered, capped, sums) = refs[:10], refs[10:20], refs[20:25]
    rows_v, weight_v, capped_v, part, row_sem, weight_sem, out_sem, capped_sem = refs[25:]
    rows, half = own[0].shape
    loads = [(hidden, rows_v.at[pl.ds(pl.multiple_of(place[0] * rows, rows), rows), :])]
    for side, blocks in ((place[8], own), (1 - place[8], other)):
        for i, block in enumerate(blocks):
            at = pl.multiple_of(place[i + 1 if i < 7 else i - 2] * rows, rows)
            left = half - block.shape[1] if i > 6 else 0
            left = pl.multiple_of(side * half + left, 128)
            loads.append((block, rows_v.at[pl.ds(at, rows), pl.ds(left, block.shape[1])]))
    loads = [pltpu.make_async_copy(a, b, row_sem.at[i]) for i, (a, b) in enumerate(loads)]
    cols = [slice(n * tile, (n + 1) * tile) for n in range(weight.shape[1] // tile)]
    weights = [
        pltpu.make_async_copy(weight.at[:, c], weight_v.at[:, c], weight_sem.at[n])
        for n, c in enumerate(cols)
    ]
    for c in weights[:1] + loads:
        c.start()
    for c in loads:
        c.wait()
    keeps = [pltpu.make_async_copy(rows_v, gathered, out_sem)]
    part[...] = jnp.zeros_like(part)
    for n, c in enumerate(cols):
        if n + 1 < len(cols):
            weights[n + 1].start()
        weights[n].wait()

        @pl.loop(0, rows_v.shape[0] // 512)
        def _(m):
            at = pl.ds(pl.multiple_of(m * 512, 512), 512)
            raw = jnp.dot(rows_v[at, :], weight_v[:, c], preferred_element_type=F32)
            cap = jnp.tanh(raw * (1.0 / 30.0))
            capped_v[at, c] = cap
            e = jnp.exp2(EXPONENT * cap)
            s = part[at, :]
            for k in range(tile // 128):
                s = s + e[:, k * 128 : (k + 1) * 128]
            part[at, :] = s

        keeps.append(
            pltpu.make_async_copy(capped_v.at[:, c], capped.at[:, c], capped_sem.at[n])
        )
        keeps[-1].start()
        if n == 0:
            keeps[0].start()
    sums[0:1, :] = jnp.sum(part[...].T, axis=0, keepdims=True)
    sums[1:2, :] = teacher_sum[...]
    for c in keeps:
        c.wait()


def scores(place, hidden, own, other, weight, teacher_sum):
    (depth, cols), tile = weight.shape, 256
    rows = 8 * hidden.shape[0]
    return pl.pallas_call(
        functools.partial(scores_kernel, tile),
        name="scores",
        out_shape=(
            jax.ShapeDtypeStruct((rows, depth), BF),
            jax.ShapeDtypeStruct((rows, cols), F32),
            jax.ShapeDtypeStruct((2, rows), F32),
        ),
        in_specs=[SMEM] + [ANY] * 22 + [VMEM],
        out_specs=(ANY, ANY, VMEM),
        scratch_shapes=[
            pltpu.VMEM((rows, depth), BF),
            pltpu.VMEM((depth, cols), BF),
            pltpu.VMEM((rows, cols), F32),
            pltpu.VMEM((rows, 128), F32),
            pltpu.SemaphoreType.DMA((21,)),
            pltpu.SemaphoreType.DMA((cols // tile,)),
            pltpu.SemaphoreType.DMA,
            pltpu.SemaphoreType.DMA((cols // tile,)),
        ],
        compiler_params=pltpu.CompilerParams(vmem_limit_bytes=VMEM_BYTES),
        cost_estimate=pl.CostEstimate(
            flops=2 * rows * depth * cols, bytes_accessed=20 << 20, transcendentals=2 * rows * cols
        ),
    )(place, hidden, *own, *other, weight, teacher_sum)


def delta_kernel(core, capped, teacher, totals, weight, delta, share, own, weight_v, sem):
    half = weight_v.shape[0]
    at = pl.ds(pl.multiple_of((1 - core[0]) * half, half), half)
    load = pltpu.make_async_copy(weight.at[at, :], weight_v, sem.at[0])
    at = pl.ds(pl.multiple_of(core[0] * half, half), half)
    ahead = pltpu.make_async_copy(weight.at[at, :], own, sem.at[1])
    i = pl.program_id(0)

    @pl.when(i == 0)
    def _():
        load.start()

    scale = (8192.0 / totals[...]).T
    cap = capped[...]
    student = jnp.exp2(EXPONENT * cap) * scale[:, 0:1]
    target = jnp.exp2(teacher[...].astype(F32) * (EXPONENT / 30.0)) * scale[:, 1:2]
    d = ((student - target) * (1.0 - cap * cap)).astype(BF)
    delta[...] = d

    @pl.when(i == 0)
    def _():
        load.wait()
        ahead.start()

    share[...] = lax.dot_general(
        d, weight_v[...], (((1,), (1,)), ((), ())), preferred_element_type=F32
    ).astype(BF)

    @pl.when(i == pl.num_programs(0) - 1)
    def _():
        ahead.wait()


def delta_and_share(core, capped, teacher, totals, weight):
    (rows, cols), half, tile = capped.shape, weight.shape[0] // 2, 256
    block = lambda shape, f: pl.BlockSpec(shape, f)
    return pl.pallas_call(
        delta_kernel,
        name="delta_and_share",
        grid_spec=pltpu.PrefetchScalarGridSpec(
            num_scalar_prefetch=1,
            grid=(rows // tile,),
            in_specs=[
                block((tile, cols), lambda i, core: (i, 0)),
                block((tile, cols), lambda i, core: (i, 0)),
                block((8, tile), lambda i, core: (0, i)),
                ANY,
            ],
            out_specs=[
                block((tile, cols), lambda i, core: (i, 0)),
                block((tile, half), lambda i, core: (i, 0)),
                ANY,
            ],
            scratch_shapes=[pltpu.VMEM((half, cols), BF), pltpu.SemaphoreType.DMA((2,))],
        ),
        out_shape=(
            jax.ShapeDtypeStruct((rows, cols), BF),
            jax.ShapeDtypeStruct((rows, half), BF),
            pltpu.VMEM((half, cols), BF),
        ),
        compiler_params=pltpu.CompilerParams(vmem_limit_bytes=36 << 20),
        cost_estimate=pl.CostEstimate(
            flops=2 * rows * half * cols, bytes_accessed=16 << 20, transcendentals=2 * rows * cols
        ),
    )(core, capped, teacher, totals, weight)


def share_kernel(delta, weight, share):
    share[...] = lax.dot_general(
        delta[...], weight[...], (((1,), (1,)), ((), ())), preferred_element_type=F32
    ).astype(BF)


def own_share(delta, weight):
    (rows, cols), half, tile = delta.shape, weight.shape[0], 256
    return pl.pallas_call(
        share_kernel,
        name="own_share",
        grid=(rows // tile,),
        in_specs=[pl.BlockSpec((tile, cols), lambda i: (i, 0)), VMEM],
        out_specs=pl.BlockSpec((tile, half), lambda i: (i, 0)),
        out_shape=jax.ShapeDtypeStruct((rows, half), BF),
        compiler_params=pltpu.CompilerParams(vmem_limit_bytes=36 << 20),
        cost_estimate=pl.CostEstimate(
            flops=2 * rows * half * cols, bytes_accessed=10 << 20, transcendentals=0
        ),
    )(delta, weight)


def chip_sum_kernel(parts, after, out, parts_v, total, sem):
    count = parts.shape[0] // sem.shape[0]
    pieces = [pl.ds(i * count, count) for i in range(sem.shape[0])]
    loads = [
        pltpu.make_async_copy(parts.at[p], parts_v.at[p], sem.at[i]) for i, p in enumerate(pieces)
    ]
    for c in loads:
        c.start()
    for i, p in enumerate(pieces):
        loads[i].wait()
        now = jnp.sum(parts_v[p].astype(F32), axis=0)
        total[...] = now if i == 0 else total[...] + now
    rows, half = out.shape[0], total.shape[1]
    for k in range(2):
        out[:, k * half : (k + 1) * half] = total[k * rows : (k + 1) * rows, :].astype(BF)


def chip_sum(parts, after):
    count, rows, cols = parts.shape
    return pl.pallas_call(
        chip_sum_kernel,
        name="chip_sum",
        in_specs=[ANY, ANY],
        out_specs=VMEM,
        out_shape=jax.ShapeDtypeStruct((rows // 2, 2 * cols), BF),
        scratch_shapes=[
            pltpu.VMEM((count, rows, cols), BF),
            pltpu.VMEM((rows, cols), F32),
            pltpu.SemaphoreType.DMA((8,)),
        ],
        compiler_params=pltpu.CompilerParams(vmem_limit_bytes=16 << 20),
        cost_estimate=pl.CostEstimate(flops=parts.size, bytes_accessed=4 << 20, transcendentals=0),
    )(parts, after)


def per_device(hidden, head_weight, teacher_logits):
    core = lax.axis_index("core")
    zh, x = lax.axis_index("zh"), lax.axis_index("x")
    vocab = lax.axis_index(("y", "zl", "core"))
    half = hidden.shape[1] // 2
    rows = 8 * hidden.shape[0]
    steps = (1, 3, 2)

    group = teacher_logits.shape[0]
    mine = jnp.sum(jnp.exp(teacher_logits.astype(F32) / 2.0), axis=1)
    teacher_sum = lax.dynamic_update_slice_in_dim(
        jnp.zeros((rows,), F32), mine, vocab * group, 0
    )
    by_owner = teacher_logits.reshape(group, 16, -1).transpose(1, 0, 2)
    teacher = lax.all_to_all(
        by_owner, ("y", "zl", "core"), split_axis=0, concat_axis=0, tiled=True
    ).reshape(rows, -1)

    cut = 768
    near = lax.dynamic_slice_in_dim(hidden, core * half, half, 1)
    far = shift(near, "zh", 2, 1)
    left = left_columns(far, cut, mine, by_owner)
    near = [shift(near, "x", 4, s) for s in steps]
    own = near + [far] + [shift(left, "x", 4, s) for s in steps]
    own += [shift(b[:, cut:], "zh", 2, 1) for b in near]
    other = [swap(b) for b in own]
    place = [zh * 4 + (x - s) % 4 for s in (0,) + steps]
    place += [(1 - zh) * 4 + (x - s) % 4 for s in (0,) + steps]
    place = jnp.stack(place + [core]).astype(jnp.int32)

    gathered, capped, sums = scores(place, hidden, own, other, head_weight, teacher_sum[None])
    totals = jnp.concatenate([total(sums), jnp.ones((6, rows), F32)])

    which = core[None].astype(jnp.int32)
    delta, give, own_weight = delta_and_share(which, capped, teacher, totals, head_weight)
    keep = own_share(delta, own_weight)
    chip = (keep.astype(F32) + swap(give).astype(F32)).astype(BF)
    parts = lax.all_to_all(
        chip.reshape(128, rows // 128, half), EVERY, split_axis=0, concat_axis=0, tiled=True
    )
    grad_head = lax.dot_general(
        gathered, delta, (((0,), (0,)), ((), ())), preferred_element_type=F32
    ).astype(BF)
    grad_hidden = chip_sum(parts.reshape(64, rows // 64, half), grad_head[:8, :128])
    return grad_hidden, grad_head


def solution(mesh):
    fine = Mesh(mesh.devices.reshape(2, 4, 4, 2, 2), ("zh", "x", "y", "zl", "core"))
    dp, vocab = ("zh", "x"), ("y", "zl", "core")
    return jax.shard_map(
        per_device,
        mesh=fine,
        in_specs=(P(dp, None), P(None, dp + vocab), P(vocab, dp)),
        out_specs=(P(dp + vocab, None), P(None, dp + vocab)),
        check_vma=False,
    )
```
